32 devices in a mesh: groups: 2 (over x), gx: 16 (over z, y, core).
Axes of the slice: x: 2, y: 2, z: 4, core: 2. Of those that a mesh axis runs over, the one named last changes fastest.
Arguments:
- right_side: float32 [256, 256, 512], P(('groups', 'gx')), parts along dimension 0, may hold values from -14 to 14
- kappa_sq: float32 [256, 256, 512], P(('groups', 'gx')), parts along dimension 0, may hold values from 0.1 to 4
- depth: int32 [256, 256], P(('groups', 'gx')), parts along dimension 0, may hold values from 128 to 512
- agg_ids: int32 [1024], P(('groups', 'gx')), parts along dimension 0, may hold values from 0 to 255, as said below
- coarse_inverse: float32 [512, 256], P('groups'), parts along dimension 0, may hold values from -3 to 3
Outputs:
- applied: float32 [256, 256, 512], P(('groups', 'gx')), parts along dimension 0
The draws below stay inside these ranges and needn't reach their ends.
There are 2 independent parts, one for each index of `groups`. The reference program is written for one: setup_inputs(seed, part) draws one part's arguments, and reference() takes and returns one part's arrays. A program takes and returns all parts, laid end to end along the dimension named above; each array names one. Nothing has to cross between parts.
Inputs may be any that keep to these rules, and one draw needn't show every extreme that they name: `agg_ids`: each aggregate 0 to 255 is named by exactly two coarse blocks.
All inputs are finite; a program needn't handle non-finite values.
Results may differ from the reference program's by a relative error of at most 0.0003.
Values sent between devices are 32-bit elements; how exact they have to be, the bound alone decides.
A program may use at most 128 MiB of HBM per device.

```python
import jax
import jax.numpy as jnp
from jax import lax

CX = 8
NY = 256
NZ = 512
MARGIN = 4
SWEEPS = 4
BY = 64
BZ = 64
BLOCK_CELLS = 32768
NB = 512
NC = 256
NX = 128
N_GX = 16


def draw_right_side(key, part):
    key = jax.random.fold_in(key, 11)
    first, second = jax.random.split(key, 2)
    slabs = NX // CX
    offsets = jax.random.normal(second, (slabs, 1, NY // BY, 1, NZ // BZ, 1), jnp.float32)
    offsets = jnp.broadcast_to(offsets, (slabs, CX, NY // BY, BY, NZ // BZ, BZ)).reshape(NX, NY, NZ)
    noise = jax.random.normal(first, (NX, NY, NZ), jnp.float32)
    values = noise + offsets
    return jnp.clip(values, -14.0, 14.0)


def draw_kappa_sq(key, part):
    key = jax.random.fold_in(key, 47)
    level = jax.random.uniform(key, (NX, NY, NZ), jnp.float32, 0.0, 1.0)
    values = 0.1 * jnp.exp(level * jnp.log(40.0))
    return jnp.clip(values, 0.1, 4.0)


def draw_agg_ids(key, part):
    key = jax.random.fold_in(key, 23)
    order = jax.random.permutation(key, NB)
    return (order % NC).astype(jnp.int32)


def draw_coarse_inverse(key, part):
    key = jax.random.fold_in(key, 37)
    first, second = jax.random.split(key)
    rows = jax.lax.broadcasted_iota(jnp.int32, (NC, NC), 0)
    cols = jax.lax.broadcasted_iota(jnp.int32, (NC, NC), 1)
    eye = (rows == cols).astype(jnp.float32)
    off = jax.random.normal(first, (NC, NC), jnp.float32) * 0.6 * (1.0 / NC) ** 0.5
    diag = jax.random.uniform(second, (NC, NC), jnp.float32, 1.0, 2.0)
    return jnp.clip(off * (1.0 - eye) + eye * diag, -3.0, 3.0)


def with_ends(entries, own_key, smallest, top_value):
    place = [jax.random.randint(jax.random.fold_in(own_key, axis), (), 0, length) for axis, length in enumerate(entries.shape)]
    longest = entries.shape.index(max(entries.shape))
    next_to = place[:longest] + [(place[longest] + 1) % entries.shape[longest]] + place[longest + 1:]
    return entries.at[tuple(place)].set(smallest).at[tuple(next_to)].set(top_value)


def setup_inputs(seed: int = 0, part: int = 0) -> dict:
    streams_of = jax.random.split(jax.random.key(seed), 6)
    own_keys = jax.random.split(jax.random.fold_in(streams_of[5], part), 6)
    right_side = draw_right_side(jax.random.fold_in(jax.random.fold_in(streams_of[5], part), 71), part)
    kappa_sq = draw_kappa_sq(jax.random.fold_in(jax.random.fold_in(streams_of[5], part), 71), part)
    depth = with_ends(jax.random.randint(own_keys[2], (NX, NY), NZ // 4, NZ + 1), jax.random.fold_in(own_keys[2], 1), NZ // 4, NZ).astype(jnp.int32)
    agg_ids = draw_agg_ids(jax.random.fold_in(jax.random.fold_in(streams_of[5], part), 71), part)
    coarse_inverse = draw_coarse_inverse(jax.random.fold_in(jax.random.fold_in(streams_of[5], part), 71), part)
    return dict(right_side=right_side, kappa_sq=kappa_sq, depth=depth, agg_ids=agg_ids, coarse_inverse=coarse_inverse)


def neighbour_sum(u):
    padded = jnp.pad(u, 1)
    total = 4.0 * (padded[2:, 1:-1, 1:-1] + padded[:-2, 1:-1, 1:-1])
    total = total + padded[1:-1, 2:, 1:-1] + padded[1:-1, :-2, 1:-1]
    total = total + padded[1:-1, 1:-1, 2:] + padded[1:-1, 1:-1, :-2]
    return total


def reference(right_side, kappa_sq, depth, agg_ids, coarse_inverse):
    depth_idx = lax.broadcasted_iota(jnp.int32, right_side.shape, 2)
    mask = (depth_idx < depth[:, :, None]).astype(jnp.float32)
    dinv = mask / (kappa_sq + 12.0)
    masked = mask * right_side
    dpad = jnp.pad(dinv, ((MARGIN, MARGIN), (0, 0), (0, 0)))

    def subdomain(index):
        start = (index * CX).astype(jnp.int32)
        ext = lax.dynamic_slice_in_dim(dpad, start, CX + 2 * MARGIN, 0)
        local_mask = (ext > 0).astype(jnp.float32)
        owned = lax.dynamic_slice_in_dim(masked, start, CX, 0)
        source = jnp.pad(owned, ((MARGIN, MARGIN), (0, 0), (0, 0)))
        field = source
        for sweep in range(SWEEPS):
            field = source + local_mask * neighbour_sum(ext * field)
        return ext * field

    pieces = lax.map(subdomain, jnp.arange(N_GX, dtype=jnp.int32))
    middle = pieces[:, MARGIN:MARGIN + CX]
    upper = pieces[:, MARGIN + CX:]
    lower = pieces[:, :MARGIN]
    zeros = jnp.zeros_like(upper[:1])
    from_left = jnp.concatenate([zeros, upper[:-1]], axis=0)
    from_right = jnp.concatenate([lower[1:], zeros], axis=0)
    fine = middle + jnp.pad(from_left, ((0, 0), (0, CX - MARGIN), (0, 0), (0, 0)))
    fine = fine + jnp.pad(from_right, ((0, 0), (CX - MARGIN, 0), (0, 0), (0, 0)))
    fine = fine.reshape(NX, NY, NZ)
    block_sums = masked.reshape(N_GX, CX, NY // BY, BY, NZ // BZ, BZ).sum(axis=(1, 3, 5)).reshape(-1) / BLOCK_CELLS
    onehot = (agg_ids[:, None] == jnp.arange(NC, dtype=jnp.int32)[None, :]).astype(jnp.float32)
    coarse_rhs = jnp.dot(block_sums, onehot, precision=lax.Precision.HIGHEST)
    coarse_sol = jnp.dot(coarse_inverse, coarse_rhs, precision=lax.Precision.HIGHEST)
    per_block = jnp.dot(onehot, coarse_sol, precision=lax.Precision.HIGHEST)
    per_block = per_block.reshape(N_GX, 1, NY // BY, 1, NZ // BZ, 1)
    coarse = jnp.broadcast_to(per_block, (N_GX, CX, NY // BY, BY, NZ // BZ, BZ)).reshape(NX, NY, NZ)
    return fine + mask * coarse
```

```python
import functools

import jax
import jax.numpy as jnp
from jax import lax
from jax.experimental import pallas as pl
from jax.experimental.pallas import tpu as pltpu
from jax.sharding import PartitionSpec as P

SWEEPS = 4
BY = 64
BZ = 64
BLOCK_CELLS = 32768
ROWS = 16
PAD = 8
LANES = 128
CHUNKS = 2
MESH = pl.DeviceIdType.MESH
HIGHEST = lax.Precision.HIGHEST


def in_plane(u, planes_at, y, first, last):
    block = u[planes_at + (pl.ds(y, ROWS + 2 * PAD), slice(None))]
    height, width = block.shape
    up = pltpu.roll(block, 1, 0)[PAD : PAD + ROWS]
    down = pltpu.roll(block, height - 1, 0)[PAD : PAD + ROWS]
    mid = block[PAD : PAD + ROWS]
    count = width // LANES
    cols = [mid[:, i * LANES : (i + 1) * LANES] for i in range(count)]
    right = [pltpu.roll(c, 1, 1) for c in cols]
    left = [pltpu.roll(c, LANES - 1, 1) for c in cols]
    zero = jnp.zeros_like(cols[0])
    below = jnp.concatenate(
        [jnp.where(first, right[i - 1] if i else zero, right[i]) for i in range(count)], axis=1
    )
    above = jnp.concatenate(
        [jnp.where(last, left[i + 1] if i + 1 < count else zero, left[i]) for i in range(count)],
        axis=1,
    )
    return (up + down) + (below + above)


def kernel(
    n, right_ref, kappa_ref, depth_ref, agg_ref, inverse_ref, out_ref,
    u, dinv, data, part, parts, in_sem, send_sem, recv_sem, part_send, part_recv, out_sem,
):
    slab, ny, nz = right_ref.shape
    me = lax.axis_index("gx")
    order = [p for pair in zip(range(slab // 2), range(slab - 1, slab // 2 - 1, -1)) for p in pair]
    loads = {}
    for p in order:
        loads[p] = [
            pltpu.make_async_copy(right_ref.at[p], data.at[p], in_sem.at[0, p]),
            pltpu.make_async_copy(kappa_ref.at[p], dinv.at[p], in_sem.at[1, p]),
        ]
        for copy in loads[p]:
            copy.start()

    barrier = pltpu.get_barrier_semaphore()

    @pl.loop(1, n)
    def _(step):
        pl.semaphore_signal(
            barrier, inc=1, device_id={"gx": lax.rem(me + step, n)}, device_id_type=MESH
        )

    lane = lax.broadcasted_iota(jnp.int32, (ROWS, LANES), 1)
    first, last = lane == 0, lane == LANES - 1
    z = lax.broadcasted_iota(jnp.int32, (ROWS, nz), 1)
    for level in range(SWEEPS):
        for p in range(slab):
            u[level, p + 1, pl.ds(0, PAD), :] = jnp.zeros((PAD, nz), jnp.float32)
            u[level, p + 1, pl.ds(PAD + ny, PAD), :] = jnp.zeros((PAD, nz), jnp.float32)

    for edge, place in ((0, 0), (n - 1, slab + 1)):

        @pl.when(me == edge)
        def _():
            for level in range(SWEEPS):

                @pl.loop(0, ny // ROWS)
                def _(tile):
                    y = pl.multiple_of(tile * ROWS, ROWS)
                    u[level, place, pl.ds(y + PAD, ROWS), :] = jnp.zeros((ROWS, nz), jnp.float32)

    height = ny // CHUNKS

    def transfer(level, side, chunk):
        rows = pl.ds(PAD + chunk * height, height)
        return pltpu.make_async_remote_copy(
            src_ref=u.at[level, slab if side else 1, rows],
            dst_ref=u.at[level, 0 if side else slab + 1, rows],
            send_sem=send_sem.at[level, side, chunk],
            recv_sem=recv_sem.at[level, side, chunk],
            device_id={"gx": lax.rem(me + (1 if side else n - 1), n)},
            device_id_type=MESH,
        )

    def sends(side):
        return me < n - 1 if side else me > 0

    def receives(side):
        return me > 0 if side else me < n - 1

    def send(level, chunk):
        for side in range(2):

            @pl.when(sends(side))
            def _():
                transfer(level, side, chunk).start()

    def await_halo(level, chunk):
        for side in range(2):

            @pl.when(receives(side))
            def _():
                transfer(level, side, chunk).wait_recv()

    def prepare(p, y, rows):
        inside = z < depth_ref[rows, p : p + 1]
        inv = jnp.where(inside, 1.0 / (dinv[p, rows, :] + 12.0), 0.0)
        masked = jnp.where(inside, data[p, rows, :], 0.0)
        dinv[p, rows, :] = inv
        u[0, p + 1, pl.ds(y + PAD, ROWS), :] = inv * masked
        return masked

    blocks_y = ny // BY
    sums = [jnp.zeros((PAD, nz), jnp.float32) for _ in range(blocks_y)]

    def fold(planes, sums):
        for p in planes:
            for copy in loads[p]:
                copy.wait()
        for j in range(blocks_y):

            def body(tile, total):
                y = pl.multiple_of(j * BY + tile * ROWS, ROWS)
                rows = pl.ds(y, ROWS)
                for p in planes:
                    masked = prepare(p, y, rows)
                    for r in range(0, ROWS, PAD):
                        total = total + masked[r : r + PAD]
                return total

            sums[j] = lax.fori_loop(0, BY // ROWS, body, sums[j])
        return sums

    sums = fold([0, slab - 1], sums)
    pl.semaphore_wait(barrier, n - 1)
    for chunk in range(CHUNKS):
        send(0, chunk)
    for pair in range(2, slab, 2):
        sums = fold(order[pair : pair + 2], sums)

    blocks_z = nz // BZ
    blocks = blocks_y * blocks_z
    count = inverse_ref.shape[0]
    onehot = (
        agg_ref[...] == lax.broadcasted_iota(jnp.int32, (blocks, count), 1)
    ).astype(jnp.float32)
    spread = (
        lax.broadcasted_iota(jnp.int32, (blocks_z, nz), 1) // BZ
        == lax.broadcasted_iota(jnp.int32, (blocks_z, nz), 0)
    ).astype(jnp.float32)
    rhs = jnp.zeros((1, count), jnp.float32)
    for j in range(blocks_y):
        row = jnp.sum(sums[j], axis=0, keepdims=True) / BLOCK_CELLS
        per_block = jnp.sum(spread * row, axis=1, keepdims=True)
        rhs = rhs + jnp.sum(onehot[j * blocks_z : (j + 1) * blocks_z] * per_block, axis=0, keepdims=True)
    part[...] = jnp.broadcast_to(rhs, part.shape)

    def part_copy(step):
        return pltpu.make_async_remote_copy(
            src_ref=part,
            dst_ref=parts.at[step],
            send_sem=part_send.at[step],
            recv_sem=part_recv.at[step],
            device_id={"gx": lax.rem(me + step, n)},
            device_id_type=MESH,
        )

    @pl.loop(1, n)
    def _(step):
        part_copy(step).start()

    def advance(level, planes, y):
        for p in planes:
            rows = pl.ds(y + PAD, ROWS)
            around = in_plane(u, (level, p + 1), y, first, last)
            across = u[level, p, rows, :] + u[level, p + 2, rows, :]
            yield p, u[0, p + 1, rows, :] + dinv[p, pl.ds(y, ROWS), :] * (around + 4.0 * across)

    def sweep(level, planes, begin, end):
        @pl.loop(begin // ROWS, end // ROWS)
        def _(tile):
            y = pl.multiple_of(tile * ROWS, ROWS)
            for p, value in advance(level, planes, y):
                u[level + 1, p + 1, pl.ds(y + PAD, ROWS), :] = value

    edges, inner = [0, slab - 1], list(range(1, slab - 1))
    for level in range(SWEEPS - 1):
        sweep(level, inner, 0, ny)
        for chunk in range(CHUNKS):
            await_halo(level, chunk)
            sweep(level, edges, chunk * height, (chunk + 1) * height)
            send(level + 1, chunk)

    @pl.loop(1, n)
    def _(step):
        part_copy(step).wait_recv()

    rhs = lax.fori_loop(1, n, lambda step, total: total + parts[step], part[...])
    solved = lax.dot_general(
        rhs, inverse_ref[...], (((1,), (1,)), ((), ())),
        precision=HIGHEST, preferred_element_type=jnp.float32,
    )[:1]
    coarse = jnp.sum(onehot * solved, axis=1, keepdims=True)
    coarse_rows = [
        jnp.sum(spread * coarse[j * blocks_z : (j + 1) * blocks_z], axis=0, keepdims=True)
        for j in range(blocks_y)
    ]

    def finish(planes, begin, end):
        for j in range(blocks_y):
            low, high = max(begin, j * BY), min(end, (j + 1) * BY)
            if low >= high:
                continue

            @pl.loop(low // ROWS, high // ROWS)
            def _(tile):
                y = pl.multiple_of(tile * ROWS, ROWS)
                rows = pl.ds(y, ROWS)
                for p, value in advance(SWEEPS - 1, planes, y):
                    inside = z < depth_ref[rows, p : p + 1]
                    data[p, rows, :] = value + jnp.where(inside, coarse_rows[j], 0.0)

    finish(inner, 0, ny)
    inner_out = pltpu.make_async_copy(
        data.at[pl.ds(1, slab - 2)], out_ref.at[pl.ds(1, slab - 2)], out_sem.at[0]
    )
    inner_out.start()
    outs = [inner_out]
    for chunk in range(CHUNKS):
        await_halo(SWEEPS - 1, chunk)
        finish(edges, chunk * height, (chunk + 1) * height)
        for p in edges:
            rows = pl.ds(chunk * height, height)
            copy = pltpu.make_async_copy(
                data.at[p, rows], out_ref.at[p, rows], out_sem.at[len(outs)]
            )
            copy.start()
            outs.append(copy)
    for copy in outs:
        copy.wait()
    for level in range(SWEEPS):
        for chunk in range(CHUNKS):
            for side in range(2):

                @pl.when(sends(side))
                def _():
                    transfer(level, side, chunk).wait_send()

    @pl.loop(1, n)
    def _(step):
        part_copy(step).wait_send()


def on_device(right_side, kappa_sq, depth, agg_ids, coarse_inverse):
    n = lax.axis_size("gx")
    slab, ny, nz = right_side.shape
    count = coarse_inverse.shape[0]
    vmem, anywhere = pl.BlockSpec(memory_space=pltpu.VMEM), pl.BlockSpec(memory_space=pl.ANY)
    return pl.pallas_call(
        functools.partial(kernel, n),
        out_shape=jax.ShapeDtypeStruct(right_side.shape, jnp.float32),
        in_specs=[anywhere, anywhere, vmem, vmem, vmem],
        out_specs=anywhere,
        scratch_shapes=[
            pltpu.VMEM((SWEEPS, slab + 2, ny + 2 * PAD, nz), jnp.float32),
            pltpu.VMEM((slab, ny, nz), jnp.float32),
            pltpu.VMEM((slab, ny, nz), jnp.float32),
            pltpu.VMEM((8, count), jnp.float32),
            pltpu.VMEM((n, 8, count), jnp.float32),
            pltpu.SemaphoreType.DMA((2, slab)),
            pltpu.SemaphoreType.DMA((SWEEPS, 2, CHUNKS)),
            pltpu.SemaphoreType.DMA((SWEEPS, 2, CHUNKS)),
            pltpu.SemaphoreType.DMA((n,)),
            pltpu.SemaphoreType.DMA((n,)),
            pltpu.SemaphoreType.DMA((1 + 2 * CHUNKS,)),
        ],
        compiler_params=pltpu.CompilerParams(
            collective_id=0, has_side_effects=True, vmem_limit_bytes=56 * 1024 * 1024
        ),
    )(right_side, kappa_sq, depth.T, agg_ids[:, None], coarse_inverse)


def solution(mesh):
    in_specs = (
        P(("groups", "gx"), None, None),
        P(("groups", "gx"), None, None),
        P(("groups", "gx"), None),
        P(("groups", "gx")),
        P("groups", None),
    )
    out_specs = P(("groups", "gx"), None, None)
    return jax.shard_map(
        on_device, mesh=mesh, in_specs=in_specs, out_specs=out_specs, check_vma=False
    )
```

```python
import functools

import jax
import jax.numpy as jnp
from jax import lax
from jax.experimental import pallas as pl
from jax.experimental.pallas import tpu as pltpu
from jax.sharding import PartitionSpec as P

SWEEPS = 4
BY = 64
BZ = 64
BLOCK_CELLS = 32768
SUB = 8
LANES = 128
CHUNKS = 2
MESH = pl.DeviceIdType.MESH
HIGHEST = lax.Precision.HIGHEST


def kernel(
    n, right_ref, kappa_ref, depth_ref, agg_ref, inverse_ref, out_ref,
    u, dinv, data, kappa, part, parts, in_sem, send_sem, recv_sem, part_send, part_recv, out_sem,
):
    slab, ny, nz = right_ref.shape
    steps, cols = ny // SUB, nz // LANES
    me = lax.axis_index("gx")
    order = [p for pair in zip(range(slab // 2), range(slab - 1, slab // 2 - 1, -1)) for p in pair]

    def column(i):
        return pl.ds(i * LANES, LANES)

    loads = {}
    for p in order:
        loads[p] = []
        for i in range(cols):
            source = (p, slice(None), column(i))
            loads[p].append(
                pltpu.make_async_copy(kappa_ref.at[source], kappa.at[p, i], in_sem.at[0, p, i])
            )
            loads[p].append(
                pltpu.make_async_copy(right_ref.at[source], data.at[p, i], in_sem.at[1, p, i])
            )
        for copy in loads[p]:
            copy.start()

    barrier = pltpu.get_barrier_semaphore()

    @pl.loop(1, n)
    def _(step):
        pl.semaphore_signal(
            barrier, inc=1, device_id={"gx": lax.rem(me + step, n)}, device_id_type=MESH
        )

    tile = (SUB, LANES)
    lane = lax.broadcasted_iota(jnp.int32, tile, 1)
    sub = lax.broadcasted_iota(jnp.int32, tile, 0)
    first, last = lane == 0, lane == LANES - 1
    top, bottom = sub == 0, sub == SUB - 1
    zero = jnp.zeros(tile, jnp.float32)

    for edge, place in ((0, 0), (n - 1, slab + 1)):

        @pl.when(me == edge)
        def _():
            @pl.loop(0, steps)
            def _(j):
                for level in range(SWEEPS):
                    for i in range(cols):
                        u[level, place, i, j + 1] = zero

    height = steps // CHUNKS

    def transfer(level, side, chunk):
        rows = pl.ds(1 + chunk * height, height)
        return pltpu.make_async_remote_copy(
            src_ref=u.at[level, slab if side else 1, :, rows],
            dst_ref=u.at[level, 0 if side else slab + 1, :, rows],
            send_sem=send_sem.at[level, side, chunk],
            recv_sem=recv_sem.at[level, side, chunk],
            device_id={"gx": lax.rem(me + (1 if side else n - 1), n)},
            device_id_type=MESH,
        )

    def sends(side):
        return me < n - 1 if side else me > 0

    def receives(side):
        return me > 0 if side else me < n - 1

    def send(level, chunk):
        for side in range(2):

            @pl.when(sends(side))
            def _():
                transfer(level, side, chunk).start()

    def await_halo(level, chunk):
        for side in range(2):

            @pl.when(receives(side))
            def _():
                transfer(level, side, chunk).wait_recv()

    def wrap(level, planes):
        for p in planes:
            for i in range(cols):
                before = pltpu.roll(u[level, p + 1, i, steps], 1, 0)
                after = pltpu.roll(u[level, p + 1, i, 1], SUB - 1, 0)
                u[level, p + 1, i, 0] = jnp.where(top, 0.0, before)
                u[level, p + 1, i, steps + 1] = jnp.where(bottom, 0.0, after)

    place = lax.broadcasted_iota(jnp.int32, (SUB, ny), 1) - steps * lax.broadcasted_iota(
        jnp.int32, (SUB, ny), 0
    )
    zs = [(lane + i * LANES).astype(jnp.float32) for i in range(cols)]

    def fold(planes, totals):
        for p in planes:
            for copy in loads[p]:
                copy.wait()
        depths = [
            jnp.broadcast_to(depth_ref[p : p + 1, :].astype(jnp.float32), (SUB, ny))
            for p in planes
        ]

        def body(j, totals):
            totals = list(totals)
            rows = pl.ds(j, SUB, stride=steps)
            for p, line in zip(planes, depths):
                depth = jnp.sum(jnp.where(place == j, line, 0.0), axis=1, keepdims=True)
                for i in range(cols):
                    inside = zs[i] < depth
                    inv = jnp.where(inside, 1.0 / (kappa[p, i, rows, :] + 12.0), 0.0)
                    masked = jnp.where(inside, data[p, i, rows, :], 0.0)
                    dinv[p, i, j] = inv
                    u[0, p + 1, i, j + 1] = inv * masked
                    totals[i] = totals[i] + masked
            return tuple(totals)

        return lax.fori_loop(0, steps, body, totals)

    edges, inner = [0, slab - 1], list(range(1, slab - 1))
    totals = fold(edges, (zero,) * cols)
    pl.semaphore_wait(barrier, n - 1)
    for chunk in range(CHUNKS):
        send(0, chunk)
    for pair in range(2, slab, 2):
        totals = fold(order[pair : pair + 2], totals)
    wrap(0, range(slab))

    blocks_y, blocks_z = ny // BY, nz // BZ
    blocks = blocks_y * blocks_z
    parts_per_block, blocks_per_col = BY // steps, LANES // BZ
    count = inverse_ref.shape[0]
    square = (blocks, blocks)
    diagonal = lax.broadcasted_iota(jnp.int32, square, 0) == lax.broadcasted_iota(
        jnp.int32, square, 1
    )
    ids = jnp.sum(
        jnp.where(diagonal, agg_ref[...].astype(jnp.float32), 0.0), axis=1, keepdims=True
    )
    onehot = (
        ids == lax.broadcasted_iota(jnp.int32, (blocks, count), 1).astype(jnp.float32)
    ).astype(jnp.float32)

    def members(j, k):
        return (sub // parts_per_block == j) & (lane // BZ == k % blocks_per_col)

    rhs = jnp.zeros((1, count), jnp.float32)
    for j in range(blocks_y):
        for k in range(blocks_z):
            picked = jnp.where(members(j, k), totals[k // blocks_per_col], 0.0)
            block = jnp.sum(jnp.sum(picked, axis=1, keepdims=True), axis=0, keepdims=True)
            b = j * blocks_z + k
            rhs = rhs + onehot[b : b + 1] * (block / BLOCK_CELLS)
    part[...] = jnp.broadcast_to(rhs, part.shape)

    def part_copy(step):
        return pltpu.make_async_remote_copy(
            src_ref=part,
            dst_ref=parts.at[step],
            send_sem=part_send.at[step],
            recv_sem=part_recv.at[step],
            device_id={"gx": lax.rem(me + step, n)},
            device_id_type=MESH,
        )

    @pl.loop(1, n)
    def _(step):
        part_copy(step).start()

    def advance(level, planes, j):
        held = {}

        def tiles(p):
            if p not in held:
                held[p] = [u[level, p, i, j + 1] for i in range(cols)]
            return held[p]

        for p in planes:
            before, mid, after = tiles(p), tiles(p + 1), tiles(p + 2)
            right = [pltpu.roll(c, 1, 1) for c in mid]
            left = [pltpu.roll(c, LANES - 1, 1) for c in mid]
            values = []
            for i in range(cols):
                below = jnp.where(first, right[i - 1] if i else zero, right[i])
                above = jnp.where(last, left[i + 1] if i + 1 < cols else zero, left[i])
                around = (u[level, p + 1, i, j] + u[level, p + 1, i, j + 2]) + (below + above)
                total = around + 4.0 * (before[i] + after[i])
                values.append(u[0, p + 1, i, j + 1] + dinv[p, i, j] * total)
            yield p, values

    def sweep(level, planes, begin, end):
        @pl.loop(begin, end)
        def _(j):
            for p, values in advance(level, planes, j):
                for i in range(cols):
                    u[level + 1, p + 1, i, j + 1] = values[i]

    for level in range(SWEEPS - 1):
        sweep(level, inner, 0, steps)
        wrap(level + 1, inner)
        for chunk in range(CHUNKS):
            await_halo(level, chunk)
            sweep(level, edges, chunk * height, (chunk + 1) * height)
            send(level + 1, chunk)
        wrap(level + 1, edges)

    @pl.loop(1, n)
    def _(step):
        part_copy(step).wait_recv()

    rhs = lax.fori_loop(1, n, lambda step, total: total + parts[step], part[...])
    solved = lax.dot_general(
        rhs, inverse_ref[...], (((1,), (1,)), ((), ())),
        precision=HIGHEST, preferred_element_type=jnp.float32,
    )[:1]
    coarse = jnp.sum(onehot * solved, axis=1, keepdims=True)
    added = [zero] * cols
    for j in range(blocks_y):
        for k in range(blocks_z):
            b, i = j * blocks_z + k, k // blocks_per_col
            added[i] = jnp.where(members(j, k), coarse[b : b + 1], added[i])

    def finish(planes, begin, end):
        @pl.loop(begin, end)
        def _(j):
            for p, values in advance(SWEEPS - 1, planes, j):
                for i in range(cols):
                    data[p, i, pl.ds(j, SUB, stride=steps), :] = values[i] + jnp.where(
                        dinv[p, i, j] > 0, added[i], 0.0
                    )

    def write(planes):
        copies = []
        for p in planes:
            for i in range(cols):
                copies.append(
                    pltpu.make_async_copy(
                        data.at[p, i], out_ref.at[p, :, column(i)], out_sem.at[p, i]
                    )
                )
                copies[-1].start()
        return copies

    finish(inner, 0, steps)
    outs = write(inner)
    for chunk in range(CHUNKS):
        await_halo(SWEEPS - 1, chunk)
        finish(edges, chunk * height, (chunk + 1) * height)
    outs += write(edges)
    for copy in outs:
        copy.wait()
    for level in range(SWEEPS):
        for chunk in range(CHUNKS):
            for side in range(2):

                @pl.when(sends(side))
                def _():
                    transfer(level, side, chunk).wait_send()

    @pl.loop(1, n)
    def _(step):
        part_copy(step).wait_send()


def on_device(right_side, kappa_sq, depth, agg_ids, coarse_inverse):
    n = lax.axis_size("gx")
    slab, ny, nz = right_side.shape
    steps, cols = ny // SUB, nz // LANES
    count = coarse_inverse.shape[0]
    vmem, anywhere = pl.BlockSpec(memory_space=pltpu.VMEM), pl.BlockSpec(memory_space=pl.ANY)
    return pl.pallas_call(
        functools.partial(kernel, n),
        out_shape=jax.ShapeDtypeStruct(right_side.shape, jnp.float32),
        in_specs=[anywhere, anywhere, vmem, vmem, vmem],
        out_specs=anywhere,
        scratch_shapes=[
            pltpu.VMEM((SWEEPS, slab + 2, cols, steps + 2, SUB, LANES), jnp.float32),
            pltpu.VMEM((slab, cols, steps, SUB, LANES), jnp.float32),
            pltpu.VMEM((slab, cols, ny, LANES), jnp.float32),
            pltpu.VMEM((slab, cols, ny, LANES), jnp.float32),
            pltpu.VMEM((8, count), jnp.float32),
            pltpu.VMEM((n, 8, count), jnp.float32),
            pltpu.SemaphoreType.DMA((2, slab, cols)),
            pltpu.SemaphoreType.DMA((SWEEPS, 2, CHUNKS)),
            pltpu.SemaphoreType.DMA((SWEEPS, 2, CHUNKS)),
            pltpu.SemaphoreType.DMA((n,)),
            pltpu.SemaphoreType.DMA((n,)),
            pltpu.SemaphoreType.DMA((slab, cols)),
        ],
        compiler_params=pltpu.CompilerParams(
            collective_id=0, has_side_effects=True, vmem_limit_bytes=56 * 1024 * 1024
        ),
    )(right_side, kappa_sq, depth, agg_ids[None, :], coarse_inverse)


def solution(mesh):
    in_specs = (
        P(("groups", "gx"), None, None),
        P(("groups", "gx"), None, None),
        P(("groups", "gx"), None),
        P(("groups", "gx")),
        P("groups", None),
    )
    out_specs = P(("groups", "gx"), None, None)
    return jax.shard_map(
        on_device, mesh=mesh, in_specs=in_specs, out_specs=out_specs, check_vma=False
    )
```

```python
import functools

import jax
import jax.numpy as jnp
from jax import lax
from jax.experimental import pallas as pl
from jax.experimental.pallas import tpu as pltpu
from jax.sharding import PartitionSpec as P

SWEEPS = 4
BY = 64
BZ = 64
BLOCK_CELLS = 32768
SUB = 8
LANES = 128
CHUNKS = 4
MESH = pl.DeviceIdType.MESH
HIGHEST = lax.Precision.HIGHEST


def kernel(
    n, right_ref, kappa_ref, depth_ref, agg_ref, inverse_ref, out_ref,
    u0, u1, u2, u3, dinv, data, kappa, part, parts, in_sem, send_sem, recv_sem, part_send, part_recv, out_sem,
):
    slab, ny, nz = right_ref.shape
    steps, cols = ny // SUB, nz // LANES
    u = (u0, u1, u2, u3)
    me = lax.axis_index("gx")
    order = [p for pair in zip(range(slab // 2), range(slab - 1, slab // 2 - 1, -1)) for p in pair]

    def column(i):
        return pl.ds(i * LANES, LANES)

    loads = {}
    for p in order:
        loads[p] = []
        for i in range(cols):
            source = (p, slice(None), column(i))
            loads[p].append(
                pltpu.make_async_copy(kappa_ref.at[source], kappa.at[p, i], in_sem.at[0, p, i])
            )
            loads[p].append(
                pltpu.make_async_copy(right_ref.at[source], data.at[p, i], in_sem.at[1, p, i])
            )
        for copy in loads[p]:
            copy.start()

    barrier = pltpu.get_barrier_semaphore()

    @pl.loop(1, n)
    def _(step):
        pl.semaphore_signal(
            barrier, inc=1, device_id={"gx": lax.rem(me + step, n)}, device_id_type=MESH
        )

    tile = (SUB, LANES)
    lane = lax.broadcasted_iota(jnp.int32, tile, 1)
    sub = lax.broadcasted_iota(jnp.int32, tile, 0)
    first, last = lane == 0, lane == LANES - 1
    top, bottom = sub == 0, sub == SUB - 1
    zero = jnp.zeros(tile, jnp.float32)

    for edge, place in ((0, 0), (n - 1, slab + 1)):

        @pl.when(me == edge)
        def _():
            @pl.loop(0, steps)
            def _(j):
                for level in range(SWEEPS):
                    for i in range(cols):
                        u[level][place, i, j + 1] = zero

    height = steps // CHUNKS

    def transfer(level, side, chunk):
        rows = pl.ds(1 + chunk * height, height)
        return pltpu.make_async_remote_copy(
            src_ref=u[level].at[slab if side else 1, :, rows],
            dst_ref=u[level].at[0 if side else slab + 1, :, rows],
            send_sem=send_sem.at[level, side, chunk],
            recv_sem=recv_sem.at[level, side, chunk],
            device_id={"gx": lax.rem(me + (1 if side else n - 1), n)},
            device_id_type=MESH,
        )

    def sends(side):
        return me < n - 1 if side else me > 0

    def receives(side):
        return me > 0 if side else me < n - 1

    def send(level, chunk):
        for side in range(2):

            @pl.when(sends(side))
            def _():
                transfer(level, side, chunk).start()

    def await_halo(level, chunk):
        for side in range(2):

            @pl.when(receives(side))
            def _():
                transfer(level, side, chunk).wait_recv()

    def wrap(level, planes):
        for p in planes:
            for i in range(cols):
                before = pltpu.roll(u[level][p + 1, i, steps], 1, 0)
                after = pltpu.roll(u[level][p + 1, i, 1], SUB - 1, 0)
                u[level][p + 1, i, 0] = jnp.where(top, 0.0, before)
                u[level][p + 1, i, steps + 1] = jnp.where(bottom, 0.0, after)

    place = lax.broadcasted_iota(jnp.int32, (SUB, ny), 1) - steps * lax.broadcasted_iota(
        jnp.int32, (SUB, ny), 0
    )
    zs = [(lane + i * LANES).astype(jnp.float32) for i in range(cols)]

    def swap(tiles):
        for d in (4, 2, 1):
            low = (sub // d) % 2 == 0
            tiles = list(tiles)
            for k in range(SUB):
                if k // d % 2 == 0:
                    x, y = tiles[k], tiles[k + d]
                    tiles[k] = jnp.where(low, x, pltpu.roll(y, d, 0))
                    tiles[k + d] = jnp.where(low, pltpu.roll(x, SUB - d, 0), y)
        return tiles

    def arrive(planes):
        for p in planes:
            for copy in loads[p]:
                copy.wait()

    def fold(planes, totals, begin, end):
        lines = [
            jnp.broadcast_to(depth_ref[p : p + 1, :].astype(jnp.float32), (SUB, ny))
            for p in planes
        ]

        def body(group, totals):
            totals = list(totals)
            j = group * SUB
            rows = [pl.ds(pl.multiple_of(s * steps + j, SUB), SUB) for s in range(SUB)]
            for p, line in zip(planes, lines):
                depths = [
                    jnp.sum(jnp.where(place == j + k, line, 0.0), axis=1, keepdims=True)
                    for k in range(SUB)
                ]
                for i in range(cols):
                    scales = swap([kappa[p, i, r, :] for r in rows])
                    values = swap([data[p, i, r, :] for r in rows])
                    for k in range(SUB):
                        inside = zs[i] < depths[k]
                        inv = jnp.where(inside, 1.0 / (scales[k] + 12.0), 0.0)
                        masked = jnp.where(inside, values[k], 0.0)
                        dinv[p, i, j + k] = inv
                        u0[p + 1, i, j + k + 1] = inv * masked
                        totals[i] = totals[i] + masked
            return tuple(totals)

        return lax.fori_loop(begin // SUB, end // SUB, body, totals)

    edges, inner = [0, slab - 1], list(range(1, slab - 1))
    totals = (zero,) * cols
    pl.semaphore_wait(barrier, n - 1)
    arrive(edges)
    for chunk in range(CHUNKS):
        totals = fold(edges, totals, chunk * height, (chunk + 1) * height)
        send(0, chunk)
    for pair in range(2, slab, 2):
        arrive(order[pair : pair + 2])
        totals = fold(order[pair : pair + 2], totals, 0, steps)
    wrap(0, range(slab))

    blocks_y, blocks_z = ny // BY, nz // BZ
    blocks = blocks_y * blocks_z
    parts_per_block, blocks_per_col = BY // steps, LANES // BZ
    count = inverse_ref.shape[0]
    square = (blocks, blocks)
    diagonal = lax.broadcasted_iota(jnp.int32, square, 0) == lax.broadcasted_iota(
        jnp.int32, square, 1
    )
    ids = jnp.sum(
        jnp.where(diagonal, agg_ref[...].astype(jnp.float32), 0.0), axis=1, keepdims=True
    )
    onehot = (
        ids == lax.broadcasted_iota(jnp.int32, (blocks, count), 1).astype(jnp.float32)
    ).astype(jnp.float32)

    def members(j, k):
        return (sub // parts_per_block == j) & (lane // BZ == k % blocks_per_col)

    rhs = jnp.zeros((1, count), jnp.float32)
    for j in range(blocks_y):
        for k in range(blocks_z):
            picked = jnp.where(members(j, k), totals[k // blocks_per_col], 0.0)
            block = jnp.sum(jnp.sum(picked, axis=1, keepdims=True), axis=0, keepdims=True)
            b = j * blocks_z + k
            rhs = rhs + onehot[b : b + 1] * (block / BLOCK_CELLS)
    part[...] = jnp.broadcast_to(rhs, part.shape)

    def part_copy(step):
        return pltpu.make_async_remote_copy(
            src_ref=part,
            dst_ref=parts.at[step],
            send_sem=part_send.at[step],
            recv_sem=part_recv.at[step],
            device_id={"gx": lax.rem(me + step, n)},
            device_id_type=MESH,
        )

    @pl.loop(1, n)
    def _(step):
        part_copy(step).start()

    def advance(level, planes, j):
        held = {}

        def tiles(p):
            if p not in held:
                held[p] = [u[level][p, i, j + 1] for i in range(cols)]
            return held[p]

        for p in planes:
            before, mid, after = tiles(p), tiles(p + 1), tiles(p + 2)
            right = [pltpu.roll(c, 1, 1) for c in mid]
            left = [pltpu.roll(c, LANES - 1, 1) for c in mid]
            values = []
            for i in range(cols):
                below = jnp.where(first, right[i - 1] if i else zero, right[i])
                above = jnp.where(last, left[i + 1] if i + 1 < cols else zero, left[i])
                around = (u[level][p + 1, i, j] + u[level][p + 1, i, j + 2]) + (below + above)
                total = around + 4.0 * (before[i] + after[i])
                values.append(u0[p + 1, i, j + 1] + dinv[p, i, j] * total)
            yield p, values

    def sweep(level, planes, begin, end):
        @pl.loop(begin, end)
        def _(j):
            for p, values in advance(level, planes, j):
                for i in range(cols):
                    u[level + 1][p + 1, i, j + 1] = values[i]

    for level in range(SWEEPS - 1):
        for chunk in range(CHUNKS):
            await_halo(level, chunk)
            sweep(level, edges, chunk * height, (chunk + 1) * height)
            send(level + 1, chunk)
            sweep(level, inner, chunk * height, (chunk + 1) * height)
        wrap(level + 1, range(slab))

    @pl.loop(1, n)
    def _(step):
        part_copy(step).wait_recv()

    rhs = lax.fori_loop(1, n, lambda step, total: total + parts[step], part[...])
    solved = lax.dot_general(
        rhs, inverse_ref[...], (((1,), (1,)), ((), ())),
        precision=HIGHEST, preferred_element_type=jnp.float32,
    )[:1]
    coarse = jnp.sum(onehot * solved, axis=1, keepdims=True)
    added = [zero] * cols
    for j in range(blocks_y):
        for k in range(blocks_z):
            b, i = j * blocks_z + k, k // blocks_per_col
            added[i] = jnp.where(members(j, k), coarse[b : b + 1], added[i])

    def finish(planes, begin, end):
        for p in planes:

            @pl.loop(begin // SUB, end // SUB)
            def _(group):
                j = group * SUB
                results = [[] for _ in range(cols)]
                for k in range(SUB):
                    for _, values in advance(SWEEPS - 1, [p], j + k):
                        for i in range(cols):
                            results[i].append(
                                values[i] + jnp.where(dinv[p, i, j + k] > 0, added[i], 0.0)
                            )
                for i in range(cols):
                    for s, value in enumerate(swap(results[i])):
                        rows = pl.ds(pl.multiple_of(s * steps + j, SUB), SUB)
                        data[p, i, rows, :] = value

    def write(planes):
        copies = []
        for p in planes:
            for i in range(cols):
                copies.append(
                    pltpu.make_async_copy(
                        data.at[p, i], out_ref.at[p, :, column(i)], out_sem.at[p, i]
                    )
                )
                copies[-1].start()
        return copies

    finish(inner, 0, steps)
    outs = write(inner)
    for chunk in range(CHUNKS):
        await_halo(SWEEPS - 1, chunk)
        finish(edges, chunk * height, (chunk + 1) * height)
    outs += write(edges)
    for copy in outs:
        copy.wait()
    for level in range(SWEEPS):
        for chunk in range(CHUNKS):
            for side in range(2):

                @pl.when(sends(side))
                def _():
                    transfer(level, side, chunk).wait_send()

    @pl.loop(1, n)
    def _(step):
        part_copy(step).wait_send()


def on_device(right_side, kappa_sq, depth, agg_ids, coarse_inverse):
    n = lax.axis_size("gx")
    slab, ny, nz = right_side.shape
    steps, cols = ny // SUB, nz // LANES
    count = coarse_inverse.shape[0]
    vmem, anywhere = pl.BlockSpec(memory_space=pltpu.VMEM), pl.BlockSpec(memory_space=pl.ANY)
    return pl.pallas_call(
        functools.partial(kernel, n),
        out_shape=jax.ShapeDtypeStruct(right_side.shape, jnp.float32),
        in_specs=[anywhere, anywhere, vmem, vmem, vmem],
        out_specs=anywhere,
        scratch_shapes=[
            *[pltpu.VMEM((slab + 2, cols, steps + 2, SUB, LANES), jnp.float32)] * SWEEPS,
            pltpu.VMEM((slab, cols, steps, SUB, LANES), jnp.float32),
            pltpu.VMEM((slab, cols, ny, LANES), jnp.float32),
            pltpu.VMEM((slab, cols, ny, LANES), jnp.float32),
            pltpu.VMEM((8, count), jnp.float32),
            pltpu.VMEM((n, 8, count), jnp.float32),
            pltpu.SemaphoreType.DMA((2, slab, cols)),
            pltpu.SemaphoreType.DMA((SWEEPS, 2, CHUNKS)),
            pltpu.SemaphoreType.DMA((SWEEPS, 2, CHUNKS)),
            pltpu.SemaphoreType.DMA((n,)),
            pltpu.SemaphoreType.DMA((n,)),
            pltpu.SemaphoreType.DMA((slab, cols)),
        ],
        compiler_params=pltpu.CompilerParams(
            collective_id=0, has_side_effects=True, vmem_limit_bytes=56 * 1024 * 1024
        ),
    )(right_side, kappa_sq, depth, agg_ids[None, :], coarse_inverse)


def solution(mesh):
    in_specs = (
        P(("groups", "gx"), None, None),
        P(("groups", "gx"), None, None),
        P(("groups", "gx"), None),
        P(("groups", "gx")),
        P("groups", None),
    )
    out_specs = P(("groups", "gx"), None, None)
    return jax.shard_map(
        on_device, mesh=mesh, in_specs=in_specs, out_specs=out_specs, check_vma=False
    )
```
